128 devices in a mesh: layer: 2 (over core), dp: 16 (over y, x), mp: 4 (over z).
Axes of the slice: x: 4, y: 4, z: 4, core: 2. Of those that a mesh axis runs over, the one named last changes fastest.
Arguments:
- grad: bfloat16 [8192, 4096], P(('layer', 'dp'), 'mp'), parts along dimension 0, may hold values from -6 to 6
- left_basis: bfloat16 [8192, 4096], P(('layer', 'mp'), 'dp'), parts along dimension 0, may hold values from -0.09375 to 0.09375
- right_basis: bfloat16 [8192, 4096], P(('layer', 'dp'), 'mp'), parts along dimension 0, may hold values from -0.09375 to 0.09375
- left_stat: float32 [8192, 4096], P(('layer', 'mp'), 'dp'), parts along dimension 0, may hold values from -6 to 6
- right_stat: float32 [8192, 4096], P(('layer', 'dp'), 'mp'), parts along dimension 0, may hold values from -6 to 6
- first_moment: float32 [8192, 4096], P(('layer', 'dp'), 'mp'), parts along dimension 0, may hold values from -6 to 6
- second_moment: float32 [8192, 4096], P(('layer', 'dp'), 'mp'), parts along dimension 0, may hold values from 0.3 to 3
Outputs:
- update: float32 [8192, 4096], P(('layer', 'dp'), 'mp'), parts along dimension 0
- left_stat_new: float32 [8192, 4096], P(('layer', 'mp'), 'dp'), parts along dimension 0
- right_stat_new: float32 [8192, 4096], P(('layer', 'dp'), 'mp'), parts along dimension 0
- first_new: float32 [8192, 4096], P(('layer', 'dp'), 'mp'), parts along dimension 0
- second_new: float32 [8192, 4096], P(('layer', 'dp'), 'mp'), parts along dimension 0
The draws below stay inside these ranges and needn't reach their ends.
There are 2 independent parts, one for each index of `layer`. The reference program is written for one: setup_inputs(seed, part) draws one part's arguments, and reference() takes and returns one part's arrays. A program takes and returns all parts, laid end to end along the dimension named above; each array names one. Nothing has to cross between parts.
All inputs are finite; a program needn't handle non-finite values.
Results may differ from the reference program's by a relative error of at most 0.022.
Values may be sent and summed in bfloat16 or wider, within the bound.
No kernel may reach another device: no remote copies, remote signals or barrier semaphores. Data moves between devices by JAX's collectives and lax.ppermute only.
A program may use at most 128 MiB of HBM per device.

```python
import math
import jax
import jax.numpy as jnp
from jax import lax

D = 4096
N_DP = 16
N_MP = 4


def shard_levels(own_key, shape, cuts, least, largest):
    def one(dim, shards_of):
        draws = jax.random.uniform(jax.random.fold_in(jax.random.fold_in(own_key, 6), dim), (shards_of,), jnp.float32, least / len(cuts), largest / len(cuts))
        return jnp.repeat(jnp.exp(draws), shape[dim] // shards_of).reshape((-1,) + (1,) * (len(shape) - dim - 1))

    level = one(*cuts[0])
    for cut in cuts[1:]:
        level = level * one(*cut)
    return level


def gaussian(key, dims, spread, bound, split=(), kind=jnp.bfloat16):
    entries = spread * jax.random.normal(key, dims, jnp.float32)
    if split:
        entries = entries * shard_levels(key, dims, split, -0.22, 0.18)
    return jnp.clip(entries, -bound, bound).astype(kind)


def setup_inputs(seed: int = 0, part: int = 0) -> dict:
    streams_of = jax.random.split(jax.random.key(seed), 8)
    own_keys = jax.random.split(jax.random.fold_in(streams_of[7], part), 8)
    grad = gaussian(own_keys[0], (D, D), 1.0, 6.0, ((0, 16), (1, 4)))
    left_basis = gaussian(own_keys[1], (D, D), D ** -0.5, 0.09375, ((0, 4), (1, 16)))
    right_basis = gaussian(own_keys[2], (D, D), D ** -0.5, 0.09375, ((0, 16), (1, 4)))
    left_stat = gaussian(own_keys[3], (D, D), 1.0, 6.0, ((0, 4), (1, 16)), jnp.float32)
    right_stat = gaussian(own_keys[4], (D, D), 1.0, 6.0, ((0, 16), (1, 4)), jnp.float32)
    first_moment = gaussian(own_keys[5], (D, D), 1.0, 6.0, ((0, 16), (1, 4)), jnp.float32)
    second_moment = jnp.clip(jnp.exp(math.log(3.0) - 2.3025851 * jax.random.uniform(own_keys[6], (D, D), jnp.float32) ** shard_levels(own_keys[6], (D, D), ((0, 16), (1, 4)), -0.2, 0.2)), 0.3, 3.0)
    return {"grad": grad, "left_basis": left_basis, "right_basis": right_basis, "left_stat": left_stat, "right_stat": right_stat, "first_moment": first_moment, "second_moment": second_moment}


stat_decay = 0.95
first_decay = 0.9
second_decay = 0.95
first_bias = 1.0 - 0.9 ** 10
second_bias = 1.0 - 0.95 ** 10
adam_eps = 1e-08

def rounded(value):
    return lax.optimization_barrier(value.astype(jnp.bfloat16)).astype(jnp.float32)

def reference(grad, left_basis, right_basis, left_stat, right_stat, first_moment, second_moment):
    col_width = D // N_MP
    row_width = D // N_DP
    left_sum = jnp.zeros((D, D), jnp.float32)
    for block in range(N_MP):
        piece = grad[:, block * col_width:(block + 1) * col_width]
        left_sum = left_sum + rounded(jnp.dot(piece, piece.T, preferred_element_type=jnp.float32))
    right_sum = jnp.zeros((D, D), jnp.float32)
    for block in range(N_DP):
        piece = grad[block * row_width:(block + 1) * row_width, :]
        right_sum = right_sum + rounded(jnp.dot(piece.T, piece, preferred_element_type=jnp.float32))
    left_stat_new = stat_decay * left_stat + (1.0 - stat_decay) * left_sum
    right_stat_new = stat_decay * right_stat + (1.0 - stat_decay) * right_sum
    half_rotated = jnp.dot(left_basis.T, grad, preferred_element_type=jnp.float32).astype(jnp.bfloat16)
    rotated = jnp.dot(half_rotated, right_basis, preferred_element_type=jnp.float32)
    first_new = first_decay * first_moment + (1.0 - first_decay) * rotated
    second_new = second_decay * second_moment + (1.0 - second_decay) * rotated * rotated
    direction = (first_new / first_bias / (jnp.sqrt(second_new / second_bias) + adam_eps)).astype(jnp.bfloat16)
    back_sum = jnp.zeros((D, D), jnp.float32)
    for block in range(N_MP):
        part_dir = direction[:, block * col_width:(block + 1) * col_width]
        part_basis = right_basis[:, block * col_width:(block + 1) * col_width]
        back_sum = back_sum + rounded(jnp.dot(part_dir, part_basis.T, preferred_element_type=jnp.float32))
    back_half = back_sum.astype(jnp.bfloat16)
    update = jnp.zeros((D, D), jnp.float32)
    for block in range(N_DP):
        part_basis = left_basis[:, block * row_width:(block + 1) * row_width]
        part_back = back_half[block * row_width:(block + 1) * row_width, :]
        update = update + rounded(jnp.dot(part_basis, part_back, preferred_element_type=jnp.float32))
    return (update, left_stat_new, right_stat_new, first_new, second_new)
```

```python
import jax
import jax.numpy as jnp
from jax import lax
from jax.experimental import pallas as pl
from jax.experimental.pallas import tpu as pltpu
from jax.sharding import PartitionSpec as P

stat_decay = 0.95
first_decay = 0.9
second_decay = 0.95
first_bias = 1.0 - 0.9**10
second_bias = 1.0 - 0.95**10
adam_eps = 1e-08

SIDE = 4
bf16, f32 = jnp.bfloat16, jnp.float32


def permute(value, target):
    pairs = []
    for y in range(SIDE):
        for x in range(SIDE):
            for z in range(SIDE):
                a, b, c = (v % SIDE for v in target(x, y, z))
                pairs.append(((y * SIDE + x) * SIDE + z, (b * SIDE + a) * SIDE + c))
    return lax.ppermute(value, ("dp", "mp"), pairs)


def shift(value, axis, by):
    dx, dy, dz = (by if axis == name else 0 for name in "xyz")
    return permute(value, lambda x, y, z: (x + dx, y + dy, z + dz))


def swap_xy(value):
    return permute(value, lambda x, y, z: (y, x, z))


def swap_xz(value):
    return permute(value, lambda x, y, z: (z, y, x))


def turn(value):
    return permute(value, lambda x, y, z: (y, z, x))


def ring_gather(value, axis):
    return [value, shift(value, axis, -1), shift(value, axis, 2), shift(value, axis, 1)]


def ring_scatter(parts, axis):
    return [
        parts[0],
        shift(parts[1], axis, 1),
        shift(parts[2], axis, 2),
        shift(parts[3], axis, -1),
    ]


def total(parts):
    return (parts[0].astype(f32) + parts[1].astype(f32)) + (parts[2].astype(f32) + parts[3].astype(f32))


def contract(left, right, left_dim, right_dim):
    return lax.dot_general(
        left, right, (((left_dim,), (right_dim,)), ((), ())), preferred_element_type=f32
    )


def rows(ref, block, size):
    return ref[pl.ds(pl.multiple_of(block * size, size), size), :]


def half_kernel(at, *refs):
    x, y, z = at[0], at[1], at[2]
    lefts, grads, outs, left_abs = refs[:4], refs[4:8], refs[8:12], refs[12]
    for i in range(4):
        left_abs[(z + i) % 4] = lefts[i][...]
    grad = jnp.concatenate([g[...] for g in grads], axis=0)
    for j in range(4):
        left = left_abs.at[(x + j) % 4]
        left = jnp.concatenate([rows(left, (y + s) % 4, 256) for s in range(4)], axis=0)
        outs[j][...] = contract(left, grad, 0, 0).astype(bf16)


def step_kernel(at, *refs):
    z = at[2]
    halves, right, first, second = refs[:4], refs[4], refs[5], refs[6]
    first_out, second_out, outs = refs[7], refs[8], refs[9:13]
    rotated = contract(halves[0][...], rows(right, z, 1024), 1, 0)
    for i in range(1, 4):
        rotated += contract(halves[i][...], rows(right, (z + i) % 4, 1024), 1, 0)
    first_new = first_decay * first[...] + (1.0 - first_decay) * rotated
    second_new = second_decay * second[...] + (1.0 - second_decay) * rotated * rotated
    first_out[...] = first_new
    second_out[...] = second_new
    direction = (first_new / first_bias / (jnp.sqrt(second_new / second_bias) + adam_eps)).astype(bf16)
    for j in range(4):
        outs[j][...] = contract(direction, rows(right, (z + j) % 4, 1024), 1, 1).astype(bf16)


def update_kernel(at, *refs):
    x, y, z = at[0], at[1], at[2]
    lefts, backs, outs, back_abs = refs[:4], refs[4:8], refs[8:12], refs[12]
    for i in range(4):
        back_abs[(x + i) % 4] = backs[i][...]
    back = jnp.concatenate([back_abs[(z + i) % 4] for i in range(4)], axis=0)
    for j in range(4):
        left = jnp.concatenate([rows(lefts[i], (y + j) % 4, 256) for i in range(4)], axis=1)
        outs[j][...] = contract(left, back, 1, 0).astype(bf16)


def left_kernel(at, *refs):
    x, y, z = at[0], at[1], at[2]
    grads, others, outs, grad_abs, other_abs = refs[:4], refs[4:8], refs[8:12], refs[12], refs[13]
    for i in range(4):
        grad_abs[pl.ds(pl.multiple_of((y + i) % 4 * 256, 256), 256), :] = grads[i][...]
        other_abs[(x + i) % 4] = others[i][...]
    for j in range(4):
        outs[j][...] = contract(grad_abs[...], other_abs[(z + j) % 4], 1, 1).astype(bf16)


def right_kernel(at, *refs):
    x, y, z = at[0], at[1], at[2]
    others, grads, outs, other_abs, grad_abs = refs[:4], refs[4:8], refs[8:12], refs[12], refs[13]
    for i in range(4):
        grad_abs[pl.ds(pl.multiple_of((y + i) % 4 * 256, 256), 256), :] = grads[i][...]
        other_abs[pl.ds(pl.multiple_of((z + i) % 4 * 256, 256), 256), :] = others[i][...]
    for j in range(4):
        columns = pl.ds(pl.multiple_of((x + j) % 4 * 256, 256), 256)
        outs[j][...] = contract(other_abs[:, columns], grad_abs[...], 0, 0).astype(bf16)


def call(kernel, name, at, operands, out_shapes, scratch=()):
    flops = 2 * 1024**3 * (2 if kernel is step_kernel else 1)
    moved = sum(v.size * v.dtype.itemsize for v in operands)
    moved += sum(v.size * v.dtype.itemsize for v in out_shapes)
    return pl.pallas_call(
        kernel,
        out_shape=out_shapes,
        in_specs=[pl.BlockSpec(memory_space=pltpu.SMEM)]
        + [pl.BlockSpec(memory_space=pltpu.VMEM)] * len(operands),
        out_specs=[pl.BlockSpec(memory_space=pltpu.VMEM)] * len(out_shapes),
        scratch_shapes=[pltpu.VMEM(s, bf16) for s in scratch],
        compiler_params=pltpu.CompilerParams(vmem_limit_bytes=48 * 1024 * 1024),
        cost_estimate=pl.CostEstimate(flops=flops, bytes_accessed=moved, transcendentals=0),
        name=name,
    )(at, *operands)


def per_device(grad, left_basis, right_basis, left_stat, right_stat, first_moment, second_moment):
    dp, z = lax.axis_index("dp"), lax.axis_index("mp")
    at = jnp.stack([dp % SIDE, dp // SIDE, z]).astype(jnp.int32)
    wide = [jax.ShapeDtypeStruct((256, 1024), bf16)] * 4
    tall = [jax.ShapeDtypeStruct((1024, 256), bf16)] * 4
    moment = [jax.ShapeDtypeStruct((256, 1024), f32)] * 2

    right_cols = lax.all_gather(right_basis, "dp", axis=0, tiled=True)
    lefts = ring_gather(swap_xz(left_basis), "z")
    grad_xz = ring_gather(swap_xy(grad), "y")
    half = call(half_kernel, "half", at, lefts + grad_xz, wide, [(4, 1024, 256)])
    half = total(ring_scatter(half, "x")).astype(bf16)
    halves = ring_gather(half, "z")
    first_new, second_new, *back = call(
        step_kernel, "step", at, halves + [right_cols, first_moment, second_moment], moment + wide
    )
    back = total(ring_scatter(back, "z")).astype(bf16)
    backs = ring_gather(back, "x")
    update = call(update_kernel, "update", at, lefts + backs, wide, [(4, 256, 1024)])
    update = swap_xy(total(ring_scatter(update, "y")).astype(bf16)).astype(f32)

    grad_yz = ring_gather(grad, "x")
    left_sum = call(left_kernel, "left_sum", at, grad_xz + grad_yz, tall, [(1024, 1024), (4, 256, 1024)])
    left_sum = swap_xz(total(ring_scatter(left_sum, "z")).astype(bf16)).astype(f32)
    left_stat_new = stat_decay * left_stat + (1.0 - stat_decay) * left_sum

    grad_xy = ring_gather(turn(grad), "z")
    right_sum = call(right_kernel, "right_sum", at, grad_xy + grad_xz, wide, [(1024, 1024)] * 2)
    right_sum = total(ring_scatter(right_sum, "x"))
    right_stat_new = stat_decay * right_stat + (1.0 - stat_decay) * right_sum
    return (update, left_stat_new, right_stat_new, first_new, second_new)


def solution(mesh):
    placed = (
        P(("layer", "dp"), "mp"),
        P(("layer", "mp"), "dp"),
        P(("layer", "dp"), "mp"),
        P(("layer", "mp"), "dp"),
        P(("layer", "dp"), "mp"),
        P(("layer", "dp"), "mp"),
        P(("layer", "dp"), "mp"),
    )
    return jax.shard_map(
        per_device,
        mesh=mesh,
        in_specs=placed,
        out_specs=(
            P(("layer", "dp"), "mp"),
            P(("layer", "mp"), "dp"),
            P(("layer", "dp"), "mp"),
            P(("layer", "dp"), "mp"),
            P(("layer", "dp"), "mp"),
        ),
        check_vma=False,
    )
```

```python
import jax
import jax.numpy as jnp
from jax import lax
from jax.experimental import pallas as pl
from jax.experimental.pallas import tpu as pltpu
from jax.sharding import PartitionSpec as P

stat_decay = 0.95
first_decay = 0.9
second_decay = 0.95
first_bias = 1.0 - 0.9**10
second_bias = 1.0 - 0.95**10
adam_eps = 1e-08

SIDE = 4
bf16, f32 = jnp.bfloat16, jnp.float32


def permute(value, target):
    pairs = []
    for layer in range(2):
        for y in range(SIDE):
            for x in range(SIDE):
                for z in range(SIDE):
                    a, b, c = (v % SIDE for v in target(layer, x, y, z))
                    pairs.append(
                        (((layer * SIDE + y) * SIDE + x) * SIDE + z, ((layer * SIDE + b) * SIDE + a) * SIDE + c)
                    )
    return lax.ppermute(value, ("layer", "dp", "mp"), pairs)


def moved(axis, by):
    def target(layer, x, y, z):
        name = {"p": "xy"[layer], "o": "yx"[layer]}.get(axis, axis)
        return (x + by * (name == "x"), y + by * (name == "y"), z + by * (name == "z"))

    return target


def shift(value, axis, by):
    return permute(value, moved(axis, by))


def ring_gather(value, axis):
    return [value, shift(value, axis, -1), shift(value, axis, 2), shift(value, axis, 1)]


def ring_scatter(parts, axis):
    return [
        parts[0],
        shift(parts[1], axis, 1),
        shift(parts[2], axis, 2),
        shift(parts[3], axis, -1),
    ]


def exchange(parts, axis):
    own, after, across, before = ring_scatter(parts, axis)
    return [own, before, across, after]


def left_blocks(parts):
    got = []
    for j, part in enumerate(parts):
        along = moved("x", j)
        got.append(
            permute(
                part,
                lambda layer, x, y, z, along=along: (x, z, y) if layer else along(layer, x, y, z),
            )
        )
    return [got[0], got[3], got[2], got[1]]


def after(value, *others):
    return lax.optimization_barrier((value, *others))[0]


def pick(value, block, dim):
    if dim == 0:
        return lax.dynamic_index_in_dim(value, block, 0, keepdims=False)
    return lax.dynamic_slice_in_dim(value, block * 256, 256, dim)


def total(parts):
    return (parts[0].astype(f32) + parts[1].astype(f32)) + (parts[2].astype(f32) + parts[3].astype(f32))


def contract(left, right, left_dim, right_dim):
    return lax.dot_general(
        left, right, (((left_dim,), (right_dim,)), ((), ())), preferred_element_type=f32
    )


def span(block):
    return pl.ds(pl.multiple_of(block % 4 * 256, 256), 256)


def place_left(at, lefts, left_abs):
    layer, p, z = at[0], at[1], at[3]
    for i in range(4):
        for s in range(4):
            row = jnp.where(layer == 0, z + i, 4 - s)
            col = jnp.where(layer == 0, p + s, z + i)
            left_abs[span(row), span(col)] = lefts[i][s]


def half_kernel(at, *refs):
    p, o = at[1], at[2]
    lefts, grads, outs, left_abs, grad_abs = refs[:4], refs[4:8], refs[8:12], refs[12], refs[13]
    place_left(at, lefts, left_abs)
    for i in range(4):
        for j in range(4):
            grad_abs[span(o + i), j * 256 : (j + 1) * 256] = grads[i][:, span(p + j)]
    for k in range(4):
        rows = slice(k * 256, (k + 1) * 256)
        half = contract(left_abs[:, rows], grad_abs[...], 0, 0).astype(bf16)
        for j in range(4):
            outs[j][rows, :] = half[:, j * 256 : (j + 1) * 256]


def rotate_kernel(at, *refs):
    p, o, z = at[1], at[2], at[3]
    halves, rights, outs, right_abs = refs[:4], refs[4:8], refs[8:12], refs[12]
    for i in range(4):
        right_abs[(o + i) % 4] = rights[i][...]
    right = jnp.concatenate([right_abs[(z + i) % 4] for i in range(4)], axis=0)
    for j in range(4):
        half = jnp.concatenate([halves[i][span(p + j), :] for i in range(4)], axis=1)
        outs[j][...] = contract(half, right, 1, 0).astype(bf16)


def back_kernel(at, *refs):
    p, o, z = at[1], at[2], at[3]
    directions, rights, outs, right_abs = refs[:4], refs[4:8], refs[8:12], refs[12]
    for i in range(4):
        right_abs[(o + i) % 4] = rights[i][...]
    direction = jnp.concatenate([d[...] for d in directions], axis=0)
    for j in range(4):
        back = contract(direction, right_abs[(z + j) % 4], 1, 1).astype(bf16)
        for i in range(4):
            outs[j][span(p + i), :] = back[i * 256 : (i + 1) * 256]


def update_kernel(at, *refs):
    p, o = at[1], at[2]
    lefts, backs, outs, left_abs, back_abs = refs[:4], refs[4:8], refs[8:12], refs[12], refs[13]
    place_left(at, lefts, left_abs)
    for i in range(4):
        back_abs[:, span(p + i)] = backs[i][...]
    for j in range(4):
        outs[j][...] = contract(left_abs[span(o + j), :], back_abs[...], 1, 0).astype(bf16)


def place_grads(at, along_o, along_p, both):
    layer, p, o = at[0], at[1], at[2]
    for i in range(4):
        both[layer, (o + i) % 4] = along_o[i][...]
        both[1 - layer, (p + i) % 4] = along_p[i][...]


def left_kernel(at, *refs):
    z, x = at[3], at[4]
    along_o, along_p, outs, both = refs[:4], refs[4:8], refs[8:12], refs[12]
    place_grads(at, along_o, along_p, both)
    for j in range(4):
        for s in range(4):
            outs[j][s] = contract(both[0, (z + j) % 4], both[1, (x + s) % 4], 1, 1).astype(bf16)


def right_kernel(at, *refs):
    z, x, y = at[3], at[4], at[5]
    others, along_o, along_p, outs, both, other_abs = refs[:4], refs[4:8], refs[8:12], refs[12:16], refs[16], refs[17]
    place_grads(at, along_o, along_p, both)
    for i in range(4):
        other_abs[(z + i) % 4] = others[i][...].reshape(1024, 256)
    grad = jnp.concatenate([both[1, (x + i) % 4] for i in range(4)], axis=0)
    for j in range(4):
        outs[j][...] = contract(other_abs[(y + j) % 4], grad, 0, 0).astype(bf16)


def left_stat_kernel(at, *refs):
    x = at[4]
    pieces, stat, out = refs[:4], refs[4], refs[5]
    for i in range(4):
        place = span(x + i)
        out[place, :] = stat_decay * stat[place, :] + (1.0 - stat_decay) * pieces[i][...].astype(f32)


def call(kernel, name, at, operands, out_shapes, scratch=()):
    flops = 2 * 1024**3
    moved = sum(v.size * v.dtype.itemsize for v in operands)
    moved += sum(v.size * v.dtype.itemsize for v in out_shapes)
    return list(pl.pallas_call(
        kernel,
        out_shape=out_shapes,
        in_specs=[pl.BlockSpec(memory_space=pltpu.SMEM)]
        + [pl.BlockSpec(memory_space=pltpu.VMEM)] * len(operands),
        out_specs=[pl.BlockSpec(memory_space=pltpu.VMEM)] * len(out_shapes),
        scratch_shapes=[pltpu.VMEM(s, bf16) for s in scratch],
        compiler_params=pltpu.CompilerParams(vmem_limit_bytes=48 * 1024 * 1024),
        cost_estimate=pl.CostEstimate(flops=flops, bytes_accessed=moved, transcendentals=0),
        name=name,
    )(at, *operands))


def per_device(grad, left_basis, right_basis, left_stat, right_stat, first_moment, second_moment):
    layer, dp, z = lax.axis_index("layer"), lax.axis_index("dp"), lax.axis_index("mp")
    x, y = dp % SIDE, dp // SIDE
    p, o = jnp.where(layer == 0, x, y), jnp.where(layer == 0, y, x)
    at = jnp.stack([layer, p, o, z, x, y]).astype(jnp.int32)
    wide = [jax.ShapeDtypeStruct((256, 1024), bf16)] * 4
    tall = [jax.ShapeDtypeStruct((1024, 256), bf16)] * 4
    cut = [jax.ShapeDtypeStruct((4, 256, 256), bf16)] * 4
    square, blocks = (1024, 1024), (4, 256, 1024)

    left = left_basis.reshape(4, 256, 256)
    left = left_blocks([pick(left, jnp.where(layer == 0, (x + j) % SIDE, j), 0) for j in range(4)])
    grads = ring_gather(grad, "o")
    lefts = ring_gather(jnp.stack(left), "z")
    right = permute(right_basis, lambda layer, x, y, z: (y, x, z) if layer else (x, y, z))
    rights = ring_gather(right, "o")
    other = exchange([pick(grad, (x + j) % SIDE, 1) for j in range(4)], "x")

    half = call(half_kernel, "half", at, lefts + grads, tall, [square, square])
    half = total(ring_scatter(half, "p")).astype(bf16)

    halves = ring_gather(after(half, *rights), "z")
    rows = ring_gather(after(grad, half), "p")

    rotated = call(rotate_kernel, "rotate", at, halves + rights, wide, [blocks])
    rotated[0] = after(rotated[0], *rows)
    rotated = total(ring_scatter(rotated, "p"))
    first_new = first_decay * first_moment + (1.0 - first_decay) * rotated
    second_new = second_decay * second_moment + (1.0 - second_decay) * rotated * rotated
    direction = (first_new / first_bias / (jnp.sqrt(second_new / second_bias) + adam_eps)).astype(bf16)
    others = ring_gather(after(jnp.stack(other), halves[1]), "z")

    directions = ring_gather(after(direction, *others), "p")
    left_sum = call(left_kernel, "left_sum", at, grads + [after(rows[0], direction)] + rows[1:], cut, [(2, *blocks)])
    left_sum = total(ring_scatter(left_sum, "z")).astype(bf16)

    back = call(back_kernel, "back", at, directions + rights, tall, [blocks])
    back[0] = after(back[0], left_sum)
    others[0] = after(others[0], directions[1])
    right_sum = call(right_kernel, "right_sum", at, others + grads + rows, wide, [(2, *blocks), (4, 1024, 256)])
    back = total(ring_scatter(back, "z")).astype(bf16)
    right_sum = ring_scatter(right_sum, "y")

    backs = ring_gather(after(back, *right_sum), "p")
    pieces = exchange([left_sum[s] for s in range(4)], "x")
    right_stat_new = stat_decay * right_stat + (1.0 - stat_decay) * total(right_sum)
    update = call(update_kernel, "update", at, lefts + backs, wide, [square, square])
    update = total(ring_scatter(update, "o"))
    left_stat_new = call(
        left_stat_kernel, "left_stat", at, pieces + [left_stat], [jax.ShapeDtypeStruct((1024, 256), f32)]
    )[0]
    return (update, left_stat_new, right_stat_new, first_new, second_new)


def solution(mesh):
    placed = (
        P(("layer", "dp"), "mp"),
        P(("layer", "mp"), "dp"),
        P(("layer", "dp"), "mp"),
        P(("layer", "mp"), "dp"),
        P(("layer", "dp"), "mp"),
        P(("layer", "dp"), "mp"),
        P(("layer", "dp"), "mp"),
    )
    return jax.shard_map(
        per_device,
        mesh=mesh,
        in_specs=placed,
        out_specs=(
            P(("layer", "dp"), "mp"),
            P(("layer", "mp"), "dp"),
            P(("layer", "dp"), "mp"),
            P(("layer", "dp"), "mp"),
            P(("layer", "dp"), "mp"),
        ),
        check_vma=False,
    )
```

```python
import jax
import jax.numpy as jnp
from jax import lax
from jax.experimental import pallas as pl
from jax.experimental.pallas import tpu as pltpu
from jax.sharding import PartitionSpec as P

stat_decay = 0.95
first_decay = 0.9
second_decay = 0.95
first_bias = 1.0 - 0.9**10
second_bias = 1.0 - 0.95**10
adam_eps = 1e-08

SIDE = 4
bf16, f32 = jnp.bfloat16, jnp.float32


def permute(value, target):
    pairs = []
    for layer in range(2):
        for y in range(SIDE):
            for x in range(SIDE):
                for z in range(SIDE):
                    a, b, c = (v % SIDE for v in target(layer, x, y, z))
                    pairs.append(
                        (((layer * SIDE + y) * SIDE + x) * SIDE + z, ((layer * SIDE + b) * SIDE + a) * SIDE + c)
                    )
    return lax.ppermute(value, ("layer", "dp", "mp"), pairs)


def moved(axis, by):
    def target(layer, x, y, z):
        name = {"p": "xy"[layer], "o": "yx"[layer]}.get(axis, axis)
        return (x + by * (name == "x"), y + by * (name == "y"), z + by * (name == "z"))

    return target


def shift(value, axis, by):
    return permute(value, moved(axis, by))


def ring_gather(value, axis):
    return [value, shift(value, axis, -1), shift(value, axis, 2), shift(value, axis, 1)]


def ring_scatter(parts, axis):
    return [
        parts[0],
        shift(parts[1], axis, 1),
        shift(parts[2], axis, 2),
        shift(parts[3], axis, -1),
    ]


def exchange(parts, axis):
    own, after, across, before = ring_scatter(parts, axis)
    return [own, before, across, after]


def left_blocks(parts):
    got = []
    for j, part in enumerate(parts):
        along = moved("x", j)
        got.append(
            permute(
                part,
                lambda layer, x, y, z, along=along: (x, z, y) if layer else along(layer, x, y, z),
            )
        )
    return [got[0], got[3], got[2], got[1]]


def after(value, *others):
    return lax.optimization_barrier((value, *others))[0]


def pick(value, block, dim):
    if dim == 0:
        return lax.dynamic_index_in_dim(value, block, 0, keepdims=False)
    return lax.dynamic_slice_in_dim(value, block * 256, 256, dim)


def total(parts):
    return (parts[0].astype(f32) + parts[1].astype(f32)) + (parts[2].astype(f32) + parts[3].astype(f32))


def contract(left, right, left_dim, right_dim):
    return lax.dot_general(
        left, right, (((left_dim,), (right_dim,)), ((), ())), preferred_element_type=f32
    )


def span(block):
    return pl.ds(pl.multiple_of(block % 4 * 256, 256), 256)


def place_left(at, lefts, left_abs):
    layer, p, z = at[0], at[1], at[3]
    for i in range(4):
        for s in range(4):
            row = jnp.where(layer == 0, z + i, 4 - s)
            col = jnp.where(layer == 0, p + s, z + i)
            left_abs[span(row), span(col)] = lefts[i][s]


def half_kernel(at, *refs):
    p, o = at[1], at[2]
    lefts, grads, outs, left_abs, grad_abs = refs[:4], refs[4:8], refs[8:12], refs[12], refs[13]
    place_left(at, lefts, left_abs)
    for i in range(4):
        for j in range(4):
            grad_abs[span(o + i), j * 256 : (j + 1) * 256] = grads[i][:, span(p + j)]
    for k in range(4):
        rows = slice(k * 256, (k + 1) * 256)
        half = contract(left_abs[:, rows], grad_abs[...], 0, 0).astype(bf16)
        for j in range(4):
            outs[j][rows, :] = half[:, j * 256 : (j + 1) * 256]


def rotate_kernel(at, *refs):
    p, o, z = at[1], at[2], at[3]
    halves, rights, outs, right_abs = refs[:4], refs[4:8], refs[8:12], refs[12]
    for i in range(4):
        right_abs[(o + i) % 4] = rights[i][...]
    right = jnp.concatenate([right_abs[(z + i) % 4] for i in range(4)], axis=0)
    for j in range(4):
        half = jnp.concatenate([halves[i][span(p + j), :] for i in range(4)], axis=1)
        outs[j][...] = contract(half, right, 1, 0).astype(bf16)


def back_kernel(at, *refs):
    p, o, z = at[1], at[2], at[3]
    directions, rights, outs, right_abs = refs[:4], refs[4:8], refs[8:12], refs[12]
    for i in range(4):
        right_abs[(o + i) % 4] = rights[i][...]
    direction = jnp.concatenate([d[...] for d in directions], axis=0)
    for j in range(4):
        back = contract(direction, right_abs[(z + j) % 4], 1, 1).astype(bf16)
        for i in range(4):
            outs[j][span(p + i), :] = back[i * 256 : (i + 1) * 256]


def update_kernel(at, *refs):
    p, o = at[1], at[2]
    lefts, backs, outs, left_abs, back_abs = refs[:4], refs[4:8], refs[8:12], refs[12], refs[13]
    place_left(at, lefts, left_abs)
    for i in range(4):
        back_abs[:, span(p + i)] = backs[i][...]
    for j in range(4):
        outs[j][...] = contract(left_abs[span(o + j), :], back_abs[...], 1, 0).astype(bf16)


def place_grads(at, along_o, along_p, both):
    layer, p, o = at[0], at[1], at[2]
    for i in range(4):
        both[layer, (o + i) % 4] = along_o[i][...]
        both[1 - layer, (p + i) % 4] = along_p[i][...]


def left_kernel(at, *refs):
    z, x = at[3], at[4]
    along_o, along_p, outs, both = refs[:4], refs[4:8], refs[8:12], refs[12]
    place_grads(at, along_o, along_p, both)
    for j in range(4):
        for s in range(4):
            outs[j][s] = contract(both[0, (z + j) % 4], both[1, (x + s) % 4], 1, 1).astype(bf16)


def right_kernel(at, *refs):
    z, x, y = at[3], at[4], at[5]
    others, along_o, along_p, outs, both, other_abs = refs[:4], refs[4:8], refs[8:12], refs[12:16], refs[16], refs[17]
    place_grads(at, along_o, along_p, both)
    for i in range(4):
        other_abs[(z + i) % 4] = others[i][...].reshape(1024, 256)
    grad = jnp.concatenate([both[1, (x + i) % 4] for i in range(4)], axis=0)
    for j in range(4):
        outs[j][...] = contract(other_abs[(y + j) % 4], grad, 0, 0).astype(bf16)


def left_stat_kernel(at, *refs):
    x = at[4]
    pieces, stat, out = refs[:4], refs[4], refs[5]
    for i in range(4):
        place = span(x + i)
        out[place, :] = stat_decay * stat[place, :] + (1.0 - stat_decay) * pieces[i][...].astype(f32)


def call(kernel, name, at, operands, out_shapes, scratch=()):
    flops = 2 * 1024**3
    moved = sum(v.size * v.dtype.itemsize for v in operands)
    moved += sum(v.size * v.dtype.itemsize for v in out_shapes)
    return list(pl.pallas_call(
        kernel,
        out_shape=out_shapes,
        in_specs=[pl.BlockSpec(memory_space=pltpu.SMEM)]
        + [pl.BlockSpec(memory_space=pltpu.VMEM)] * len(operands),
        out_specs=[pl.BlockSpec(memory_space=pltpu.VMEM)] * len(out_shapes),
        scratch_shapes=[pltpu.VMEM(s, bf16) for s in scratch],
        compiler_params=pltpu.CompilerParams(vmem_limit_bytes=48 * 1024 * 1024),
        cost_estimate=pl.CostEstimate(flops=flops, bytes_accessed=moved, transcendentals=0),
        name=name,
    )(at, *operands))


def per_device(grad, left_basis, right_basis, left_stat, right_stat, first_moment, second_moment):
    layer, dp, z = lax.axis_index("layer"), lax.axis_index("dp"), lax.axis_index("mp")
    x, y = dp % SIDE, dp // SIDE
    p, o = jnp.where(layer == 0, x, y), jnp.where(layer == 0, y, x)
    at = jnp.stack([layer, p, o, z, x, y]).astype(jnp.int32)
    wide = [jax.ShapeDtypeStruct((256, 1024), bf16)] * 4
    tall = [jax.ShapeDtypeStruct((1024, 256), bf16)] * 4
    cut = [jax.ShapeDtypeStruct((4, 256, 256), bf16)] * 4
    square, blocks = (1024, 1024), (4, 256, 1024)

    scope = jax.named_scope
    with scope("grad_o"):
        grads = ring_gather(grad, "o")
    with scope("left_blocks"):
        left = left_basis.reshape(4, 256, 256)
        left = left_blocks([pick(left, jnp.where(layer == 0, (x + j) % SIDE, j), 0) for j in range(4)])
    with scope("left_z"):
        lefts = ring_gather(jnp.stack(left), "z")
    held, right = lax.optimization_barrier((grad, right_basis, left[1]))[:2]
    with scope("right_swap"):
        right = permute(right, lambda layer, x, y, z: (y, x, z) if layer else (x, y, z))
    with scope("other_x"):
        other = exchange([pick(held, (x + j) % SIDE, 1) for j in range(4)], "x")

    lefts[0] = after(lefts[0], *other)
    half = call(half_kernel, "half", at, lefts + grads, tall, [square, square])
    with scope("half_p"):
        half = ring_scatter(half, "p")
        half[0] = after(half[0], right)
        half = total(half).astype(bf16)

    with scope("half_z"):
        halves = ring_gather(half, "z")
    held, right = lax.optimization_barrier((grad, right, half))[:2]
    with scope("right_o"):
        rights = ring_gather(right, "o")
    with scope("rows_p"):
        rows = ring_gather(held, "p")

    rotated = call(rotate_kernel, "rotate", at, halves + rights, wide, [blocks])
    with scope("rotated_p"):
        rotated = ring_scatter(rotated, "p")
        rotated[0] = after(rotated[0], *rows)
        rotated = total(rotated)
    first_new = first_decay * first_moment + (1.0 - first_decay) * rotated
    second_new = second_decay * second_moment + (1.0 - second_decay) * rotated * rotated
    direction = (first_new / first_bias / (jnp.sqrt(second_new / second_bias) + adam_eps)).astype(bf16)
    with scope("other_z"):
        others = ring_gather(after(jnp.stack(other), *halves), "z")

    with scope("direction_p"):
        directions = ring_gather(direction, "p")
    left_sum = call(left_kernel, "left_sum", at, grads + rows, cut, [(2, *blocks)])

    directions[0] = after(directions[0], *others, left_sum[0])
    back = call(back_kernel, "back", at, directions + rights, tall, [blocks])
    right_sum = call(right_kernel, "right_sum", at, others + grads + rows, wide, [(2, *blocks), (4, 1024, 256)])
    with scope("back_z"):
        back = ring_scatter(back, "z")
    with scope("right_sum_y"):
        right_sum = ring_scatter(right_sum, "y")
    back[0] = after(back[0], right_sum[0])
    back = total(back).astype(bf16)

    with scope("back_p"):
        backs = ring_gather(back, "p")
    with scope("left_sum_z"):
        left_sum = ring_scatter([after(part, back) for part in left_sum], "z")
    backs[0] = after(backs[0], *right_sum)
    update = call(update_kernel, "update", at, lefts + backs, wide, [square, square])
    left_sum[0] = after(left_sum[0], update[0])
    left_sum = total(left_sum).astype(bf16)
    with scope("update_o"):
        update = ring_scatter(update, "o")
    right_stat_new = stat_decay * right_stat + (1.0 - stat_decay) * total(right_sum)
    with scope("left_sum_x"):
        pieces = exchange([left_sum[s] for s in range(4)], "x")
    update = total(update)
    pieces[0] = after(pieces[0], update)
    left_stat_new = call(
        left_stat_kernel, "left_stat", at, pieces + [left_stat], [jax.ShapeDtypeStruct((1024, 256), f32)]
    )[0]
    return (update, left_stat_new, right_stat_new, first_new, second_new)


def solution(mesh):
    placed = (
        P(("layer", "dp"), "mp"),
        P(("layer", "mp"), "dp"),
        P(("layer", "dp"), "mp"),
        P(("layer", "mp"), "dp"),
        P(("layer", "dp"), "mp"),
        P(("layer", "dp"), "mp"),
        P(("layer", "dp"), "mp"),
    )
    return jax.shard_map(
        per_device,
        mesh=mesh,
        in_specs=placed,
        out_specs=(
            P(("layer", "dp"), "mp"),
            P(("layer", "mp"), "dp"),
            P(("layer", "dp"), "mp"),
            P(("layer", "dp"), "mp"),
            P(("layer", "dp"), "mp"),
        ),
        check_vma=False,
    )
```

```python
import jax
import jax.numpy as jnp
from jax import lax
from jax.experimental import pallas as pl
from jax.experimental.pallas import tpu as pltpu
from jax.sharding import PartitionSpec as P

stat_decay = 0.95
first_decay = 0.9
second_decay = 0.95
first_bias = 1.0 - 0.9**10
second_bias = 1.0 - 0.95**10
adam_eps = 1e-08

SIDE = 4
bf16, f32 = jnp.bfloat16, jnp.float32


def permute(value, target):
    pairs = []
    for layer in range(2):
        for y in range(SIDE):
            for x in range(SIDE):
                for z in range(SIDE):
                    a, b, c = (v % SIDE for v in target(layer, x, y, z))
                    pairs.append(
                        (((layer * SIDE + y) * SIDE + x) * SIDE + z, ((layer * SIDE + b) * SIDE + a) * SIDE + c)
                    )
    return lax.ppermute(value, ("layer", "dp", "mp"), pairs)


def moved(axis, by):
    def target(layer, x, y, z):
        name = {"p": "xy"[layer], "o": "yx"[layer]}.get(axis, axis)
        return (x + by * (name == "x"), y + by * (name == "y"), z + by * (name == "z"))

    return target


def shift(value, axis, by):
    return permute(value, moved(axis, by))


def ring_gather(value, axis):
    return [value, shift(value, axis, -1), shift(value, axis, 2), shift(value, axis, 1)]


def ring_scatter(parts, axis):
    return [
        parts[0],
        shift(parts[1], axis, 1),
        shift(parts[2], axis, 2),
        shift(parts[3], axis, -1),
    ]


def exchange(parts, axis):
    own, after, across, before = ring_scatter(parts, axis)
    return [own, before, across, after]


def left_blocks(parts):
    got = []
    for j, part in enumerate(parts):
        along = moved("x", j)
        got.append(
            permute(
                part,
                lambda layer, x, y, z, along=along: (x, z, y) if layer else along(layer, x, y, z),
            )
        )
    return [got[0], got[3], got[2], got[1]]


def after(value, *others):
    return lax.optimization_barrier((value, *others))[0]


def pick(value, block, dim):
    if dim == 0:
        return lax.dynamic_index_in_dim(value, block, 0, keepdims=False)
    return lax.dynamic_slice_in_dim(value, block * 256, 256, dim)


def total(parts):
    return (parts[0].astype(f32) + parts[1].astype(f32)) + (parts[2].astype(f32) + parts[3].astype(f32))


def contract(left, right, left_dim, right_dim):
    return lax.dot_general(
        left, right, (((left_dim,), (right_dim,)), ((), ())), preferred_element_type=f32
    )


def span(block):
    return pl.ds(pl.multiple_of(block % 4 * 256, 256), 256)


def place_left(at, lefts, left_abs):
    layer, p, z = at[0], at[1], at[3]
    for i in range(4):
        for s in range(4):
            row = jnp.where(layer == 0, z + i, 4 - s)
            col = jnp.where(layer == 0, p + s, z + i)
            left_abs[span(row), span(col)] = lefts[i][s]


def half_kernel(at, *refs):
    p, o = at[1], at[2]
    lefts, grads, outs, left_abs, grad_abs = refs[:4], refs[4:8], refs[8:12], refs[12], refs[13]
    place_left(at, lefts, left_abs)
    for i in range(4):
        for j in range(4):
            grad_abs[span(o + i), j * 256 : (j + 1) * 256] = grads[i][:, span(p + j)]
    for k in range(4):
        rows = slice(k * 256, (k + 1) * 256)
        half = contract(left_abs[:, rows], grad_abs[...], 0, 0).astype(bf16)
        for j in range(4):
            outs[j][rows, :] = half[:, j * 256 : (j + 1) * 256]


def rotate_kernel(at, *refs):
    p, o, z = at[1], at[2], at[3]
    halves, rights, outs, right_abs = refs[:4], refs[4:8], refs[8:12], refs[12]
    for i in range(4):
        right_abs[(o + i + 4 - z) % 4] = rights[i][...]
    right = right_abs[...].reshape(1024, 1024)
    for j in range(4):
        half = jnp.concatenate([halves[i][span(p + j), :] for i in range(4)], axis=1)
        outs[j][...] = contract(half, right, 1, 0).astype(bf16)


def back_kernel(at, *refs):
    p, o, z = at[1], at[2], at[3]
    directions, rights, outs, right_abs = refs[:4], refs[4:8], refs[8:12], refs[12]
    for i in range(4):
        right_abs[(o + i + 4 - z) % 4] = rights[i][...]
    direction = jnp.concatenate([d[...] for d in directions], axis=0)
    for j in range(4):
        back = contract(direction, right_abs[j], 1, 1).astype(bf16)
        for i in range(4):
            outs[j][span(p + i), :] = back[i * 256 : (i + 1) * 256]


def update_kernel(at, *refs):
    p, o = at[1], at[2]
    lefts, backs, outs, left_abs, back_abs = refs[:4], refs[4:8], refs[8:12], refs[12], refs[13]
    place_left(at, lefts, left_abs)
    for i in range(4):
        back_abs[:, span(p + i)] = backs[i][...]
    for j in range(4):
        outs[j][...] = contract(left_abs[span(o + j), :], back_abs[...], 1, 0).astype(bf16)


def place_grads(at, along_o, along_p, both):
    layer, p, o = at[0], at[1], at[2]
    for i in range(4):
        both[layer, (o + i) % 4] = along_o[i][...]
        both[1 - layer, (p + i) % 4] = along_p[i][...]


def left_kernel(at, *refs):
    z, x = at[3], at[4]
    along_o, along_p, outs, both = refs[:4], refs[4:8], refs[8:12], refs[12]
    place_grads(at, along_o, along_p, both)
    for j in range(4):
        for s in range(4):
            outs[j][s] = contract(both[0, (z + j) % 4], both[1, (x + s) % 4], 1, 1).astype(bf16)


def right_kernel(at, *refs):
    z, x, y = at[3], at[4], at[5]
    others, along_o, along_p, outs, both, other_abs = refs[:4], refs[4:8], refs[8:12], refs[12:16], refs[16], refs[17]
    place_grads(at, along_o, along_p, both)
    for i in range(4):
        other_abs[(z + i) % 4] = others[i][...].reshape(1024, 256)
    grad = jnp.concatenate([both[1, (x + i) % 4] for i in range(4)], axis=0)
    for j in range(4):
        outs[j][...] = contract(other_abs[(y + j) % 4], grad, 0, 0).astype(bf16)


def left_stat_kernel(at, *refs):
    x = at[4]
    pieces, stat, out = refs[:4], refs[4], refs[5]
    for i in range(4):
        place = span(x + i)
        out[place, :] = stat_decay * stat[place, :] + (1.0 - stat_decay) * pieces[i][...].astype(f32)


def call(kernel, name, at, operands, out_shapes, scratch=()):
    flops = 4 * 1024**3
    moved = sum(v.size * v.dtype.itemsize for v in operands)
    moved += sum(v.size * v.dtype.itemsize for v in out_shapes)
    return list(pl.pallas_call(
        kernel,
        out_shape=out_shapes,
        in_specs=[pl.BlockSpec(memory_space=pltpu.SMEM)]
        + [pl.BlockSpec(memory_space=pltpu.VMEM)] * len(operands),
        out_specs=[pl.BlockSpec(memory_space=pltpu.VMEM)] * len(out_shapes),
        scratch_shapes=[pltpu.VMEM(s, bf16) for s in scratch],
        compiler_params=pltpu.CompilerParams(vmem_limit_bytes=48 * 1024 * 1024),
        cost_estimate=pl.CostEstimate(flops=flops, bytes_accessed=moved, transcendentals=0),
        name=name,
    )(at, *operands))


def per_device(grad, left_basis, right_basis, left_stat, right_stat, first_moment, second_moment):
    layer, dp, z = lax.axis_index("layer"), lax.axis_index("dp"), lax.axis_index("mp")
    x, y = dp % SIDE, dp // SIDE
    p, o = jnp.where(layer == 0, x, y), jnp.where(layer == 0, y, x)
    at = jnp.stack([layer, p, o, z, x, y]).astype(jnp.int32)
    wide = [jax.ShapeDtypeStruct((256, 1024), bf16)] * 4
    tall = [jax.ShapeDtypeStruct((1024, 256), bf16)] * 4
    cut = [jax.ShapeDtypeStruct((4, 256, 256), bf16)] * 4
    square, blocks = (1024, 1024), (4, 256, 1024)

    scope = jax.named_scope
    with scope("grad_o"):
        grads = ring_gather(grad, "o")
    with scope("left_blocks"):
        left = left_basis.reshape(4, 256, 256)
        left = left_blocks([pick(left, jnp.where(layer == 0, (x + j) % SIDE, j), 0) for j in range(4)])
    with scope("left_z"):
        lefts = ring_gather(jnp.stack(left), "z")
    held, right = lax.optimization_barrier((grad, right_basis, left[1]))[:2]
    with scope("right_swap"):
        right = permute(right, lambda layer, x, y, z: (y, x, z) if layer else (x, y, z))
    with scope("other_x"):
        other = exchange([pick(held, (x + j) % SIDE, 1) for j in range(4)], "x")

    lefts[0] = after(lefts[0], *other)
    half = call(half_kernel, "half", at, lefts + grads, tall, [square, square])
    with scope("half_p"):
        half = ring_scatter(half, "p")
        half[0] = after(half[0], right)
        half = total(half).astype(bf16)

    with scope("half_z"):
        halves = ring_gather(half, "z")
    held, right = lax.optimization_barrier((grad, right, half))[:2]
    with scope("right_o"):
        rights = ring_gather(right, "o")
    with scope("rows_p"):
        rows = ring_gather(held, "p")

    rotated = call(rotate_kernel, "rotate", at, halves + rights, wide, [blocks])
    with scope("rotated_p"):
        rotated = ring_scatter(rotated, "p")
        rotated[0] = after(rotated[0], *rows)
        rotated = total(rotated)
    first_new = first_decay * first_moment + (1.0 - first_decay) * rotated
    second_new = second_decay * second_moment + (1.0 - second_decay) * rotated * rotated
    direction = (first_new / first_bias / (jnp.sqrt(second_new / second_bias) + adam_eps)).astype(bf16)
    with scope("other_z"):
        others = ring_gather(after(jnp.stack(other), *halves), "z")

    with scope("direction_p"):
        directions = ring_gather(direction, "p")
    left_sum = call(left_kernel, "left_sum", at, grads + rows, cut, [(2, *blocks)])

    directions[0] = after(directions[0], *others, left_sum[0])
    back = call(back_kernel, "back", at, directions + rights, tall, [blocks])
    right_sum = call(right_kernel, "right_sum", at, others + grads + rows, wide, [(2, *blocks), (4, 1024, 256)])
    with scope("back_z"):
        back = ring_scatter(back, "z")
    with scope("right_sum_y"):
        right_sum = ring_scatter(right_sum, "y")
    back[0] = after(back[0], right_sum[0])
    back = total(back).astype(bf16)

    with scope("back_p"):
        backs = ring_gather(back, "p")
    with scope("left_sum_z"):
        left_sum = ring_scatter([after(part, back) for part in left_sum], "z")
    backs[0] = after(backs[0], *right_sum)
    update = call(update_kernel, "update", at, lefts + backs, wide, [square, square])
    left_sum[0] = after(left_sum[0], update[0])
    left_sum = total(left_sum).astype(bf16)
    with scope("update_o"):
        update = ring_scatter(update, "o")
    right_stat_new = stat_decay * right_stat + (1.0 - stat_decay) * total(right_sum)
    with scope("left_sum_x"):
        pieces = exchange([left_sum[s] for s in range(4)], "x")
    update = total(update)
    pieces[0] = after(pieces[0], update)
    left_stat_new = call(
        left_stat_kernel, "left_stat", at, pieces + [left_stat], [jax.ShapeDtypeStruct((1024, 256), f32)]
    )[0]
    return (update, left_stat_new, right_stat_new, first_new, second_new)


def solution(mesh):
    placed = (
        P(("layer", "dp"), "mp"),
        P(("layer", "mp"), "dp"),
        P(("layer", "dp"), "mp"),
        P(("layer", "mp"), "dp"),
        P(("layer", "dp"), "mp"),
        P(("layer", "dp"), "mp"),
        P(("layer", "dp"), "mp"),
    )
    return jax.shard_map(
        per_device,
        mesh=mesh,
        in_specs=placed,
        out_specs=(
            P(("layer", "dp"), "mp"),
            P(("layer", "mp"), "dp"),
            P(("layer", "dp"), "mp"),
            P(("layer", "dp"), "mp"),
            P(("layer", "dp"), "mp"),
        ),
        check_vma=False,
    )
```
